32 devices in a mesh: tiles: 8 (over z, x), cams: 4 (over y, core).
Axes of the slice: x: 2, y: 2, z: 4, core: 2. Of those that a mesh axis runs over, the one named last changes fastest.
Arguments:
- offsets: float32 [2, 8192], P(None, ('tiles', 'cams')), may hold values from -6 to 6
- factor_diag: float32 [2, 8192], P(None, ('tiles', 'cams')), may hold values from 0.8 to 4
- factor_off: float32 [8192], P(('tiles', 'cams')), may hold values from -4 to 4
- logit: float32 [8192], P(('tiles', 'cams')), may hold values from -6 to 6
- appearance: float32 [19, 8192], P(None, ('tiles', 'cams')), may hold values from -6 to 6
- cam_linear: float32 [4, 4], P('cams'), may hold values from -0.3 to 0.3
- cam_shift: float32 [4, 2], P('cams'), may hold values from -2 to 2
- block_lists: int32 [4, 128, 2, 3], P('cams', 'tiles'), may hold values from 0 to 1023, as said below
- pix_grad: bfloat16 [19, 4, 32768], P(None, 'cams', 'tiles'), may hold values from -6 to 6
Outputs:
- rendered: float32 [19, 4, 32768], P(None, 'cams', 'tiles')
- grad_geometry: float32 [6, 8192], P(None, ('tiles', 'cams'))
- grad_appearance: float32 [19, 8192], P(None, ('tiles', 'cams'))
The draws below stay inside these ranges and needn't reach their ends.
Inputs may be any that keep to these rules, and one draw needn't show every extreme that they name: `block_lists`: call blocks k * 128 to (k+1) * 128 - 1 column k. For each camera and each aligned run of 16 tiles (the tiles of one device), at most 24 list entries of both slabs together name blocks of one column, and exactly 24 name blocks of some column.
All inputs are finite; a program needn't handle non-finite values.
Results may differ from the reference program's by a relative error of at most 0.012.
The reference program's roundings to bfloat16 on the way count: a program that leaves them out, or rounds other values in their place, can miss the bound.
Values may be sent and summed in bfloat16 or wider, within the bound.
A program may use at most 64 MiB of HBM per device.

```python
import math
import jax
import jax.numpy as jnp
from jax import lax

SIDE = 16
TPD = 16
LIST = 3
BLK = 8
FEAT = 19
CAMS = 4
COLUMNS = 8
ITILES = 128
PIX = 256
CAP = 24
COLBLK = 128
NG = 8192


def draw_block_lists(key, part):
    key_full, key_score, key_order, key_block = jax.random.split(key, 4)
    slot_total = COLUMNS * CAP
    entry_total = 2 * TPD * LIST
    slot_ids = jnp.arange(slot_total, dtype=jnp.int32)
    slot_column = slot_ids // CAP
    filled = jax.random.randint(key_full, (CAMS, COLUMNS, 1), 0, COLUMNS)
    score = jax.random.randint(key_score, (CAMS, COLUMNS, slot_total), 0, 2 ** 20) * slot_total + slot_ids
    score = jnp.where(slot_column[None, None, :] == filled, slot_ids - slot_total - 1, score)
    chosen = jnp.argsort(score, axis=-1, stable=True)[..., :entry_total]
    entry_ids = jnp.arange(entry_total, dtype=jnp.int32)
    mixing = jax.random.randint(key_order, (CAMS, COLUMNS, entry_total), 0, 2 ** 20) * entry_total + entry_ids
    order = jnp.argsort(mixing, axis=-1, stable=True)
    slots = jnp.take_along_axis(chosen, order, axis=-1)
    column = slots // CAP
    in_column = jax.random.randint(key_block, (CAMS, COLUMNS, entry_total), 0, COLBLK)
    block_ids = column * COLBLK + in_column
    return block_ids.reshape(CAMS, ITILES, 2, LIST).astype(jnp.int32)


def levels(key, shape, cuts, low, high):
    def one(dim, parts):
        draws = jax.random.uniform(jax.random.fold_in(jax.random.fold_in(key, 6), dim), (parts,), jnp.float32, low / len(cuts), high / len(cuts))
        return jnp.repeat(jnp.exp(draws), shape[dim] // parts).reshape((-1,) + (1,) * (len(shape) - dim - 1))

    loudness = one(*cuts[0])
    for cut in cuts[1:]:
        loudness = loudness * one(*cut)
    return loudness


def scatter_about(stream_key, dims, width, bound, shards=(), held_as=jnp.bfloat16):
    array = jax.random.normal(stream_key, dims, jnp.float32) * width
    if len(shards) > 0:
        array = levels(stream_key, dims, shards, -0.22, 0.18) * array
    return jnp.clip(array, min=-bound, max=bound).astype(held_as)


def setup_inputs(seed: int = 0) -> dict:
    streams_of = jax.random.split(jax.random.key(seed), 10)
    offsets = jnp.clip(jax.random.uniform(streams_of[0], (2, NG), jnp.float32, -6.0, 6.0) * levels(streams_of[0], (2, NG), ((1, 32),), -0.4, 0.0), -6.0, 6.0)
    factor_diag = jnp.clip(jnp.exp(math.log(4.0) - 1.609438 * jax.random.uniform(streams_of[1], (2, NG), jnp.float32) ** levels(streams_of[1], (2, NG), ((1, 32),), -0.2, 0.2)), 0.8, 4.0)
    factor_off = scatter_about(streams_of[2], (NG,), 1.0, 4.0, ((0, 32),), jnp.float32)
    logit = scatter_about(streams_of[3], (NG,), 1.5, 6.0, ((0, 32),), jnp.float32)
    appearance = scatter_about(streams_of[4], (FEAT, NG), 1.0, 6.0, ((1, 32),), jnp.float32)
    cam_linear = jnp.clip(jax.random.uniform(streams_of[5], (CAMS, 4), jnp.float32, -0.3, 0.3) * levels(streams_of[5], (CAMS, 4), ((0, 4),), -0.4, 0.0), -0.3, 0.3)
    cam_shift = jnp.clip(jax.random.uniform(streams_of[6], (CAMS, 2), jnp.float32, -2.0, 2.0) * levels(streams_of[6], (CAMS, 2), ((0, 4),), -0.4, 0.0), -2.0, 2.0)
    block_lists = draw_block_lists(jax.random.fold_in(streams_of[9], 71), 0)
    pix_grad = scatter_about(streams_of[8], (FEAT, CAMS, ITILES * PIX), 1.0, 6.0, ((1, 4), (2, 8)))
    return dict(offsets=offsets, factor_diag=factor_diag, factor_off=factor_off, logit=logit, appearance=appearance, cam_linear=cam_linear, cam_shift=cam_shift, block_lists=block_lists, pix_grad=pix_grad)


def to_half(values):
    rounded = lax.optimization_barrier(values.astype(jnp.bfloat16))
    return rounded.astype(jnp.float32)

def project(geometry, linear, camera_shift):
    lin_xx = 1.0 + linear[0]
    lin_xy = linear[1]
    lin_yx = linear[2]
    lin_yy = 1.0 + linear[3]
    diag_x = geometry[2]
    diag_y = geometry[3]
    lower = geometry[4]
    cov_xx = diag_x * diag_x
    cov_xy = diag_x * lower
    cov_yy = lower * lower + diag_y * diag_y
    half_xx = lin_xx * cov_xx + lin_xy * cov_xy
    half_xy = lin_xx * cov_xy + lin_xy * cov_yy
    half_yx = lin_yx * cov_xx + lin_yy * cov_xy
    half_yy = lin_yx * cov_xy + lin_yy * cov_yy
    img_xx = half_xx * lin_xx + half_xy * lin_xy + 0.3
    img_xy = half_xx * lin_yx + half_xy * lin_yy
    img_yy = half_yx * lin_yx + half_yy * lin_yy + 0.3
    determ = img_xx * img_yy - img_xy * img_xy
    centre_x = lin_xx * geometry[0] + lin_xy * geometry[1] + camera_shift[0]
    centre_y = lin_yx * geometry[0] + lin_yy * geometry[1] + camera_shift[1]
    opacity = 0.95 * jax.nn.sigmoid(geometry[5])
    return jnp.stack([centre_x, centre_y, img_yy / determ, -img_xy / determ, img_xx / determ, opacity])

def render_tile(projected, colours):
    pixels = jnp.arange(SIDE * SIDE)
    across = (pixels % SIDE).astype(jnp.float32) + 0.5 - SIDE / 2
    downward = (pixels // SIDE).astype(jnp.float32) + 0.5 - SIDE / 2
    delta_x = across[None, :] - projected[0][:, None]
    delta_y = downward[None, :] - projected[1][:, None]
    quadric = projected[2][:, None] * delta_x * delta_x + 2.0 * projected[3][:, None] * delta_x * delta_y + projected[4][:, None] * delta_y * delta_y
    coverage = projected[5][:, None] * jnp.exp(-0.5 * quadric)
    log_keep = jnp.log1p(-coverage)
    weight = jnp.exp(jnp.cumsum(log_keep, axis=0) - log_keep) * coverage
    return jnp.dot(colours, weight, precision=lax.Precision.HIGHEST, preferred_element_type=jnp.float32)

def tile_grads(projected, colours, cotangent):
    per_tile = projected.shape[1] // TPD
    channels = colours.shape[0]
    proj_tiles = projected.reshape(6, TPD, per_tile)
    colour_tiles = colours.reshape(channels, TPD, per_tile)

    def forward(proj_arg, colour_arg):
        return jax.vmap(render_tile, in_axes=(1, 1), out_axes=1)(proj_arg, colour_arg)
    picture, pullback = jax.vjp(forward, proj_tiles, colour_tiles)
    grad_proj, grad_colour = pullback(cotangent)
    return (picture, grad_proj.reshape(6, -1), grad_colour.reshape(channels, -1))

def reference(offsets, factor_diag, factor_off, logit, appearance, cam_linear, cam_shift, block_lists, pix_grad):
    geometry = jnp.concatenate([offsets, factor_diag, factor_off[None, :], logit[None, :]], axis=0)
    channels = appearance.shape[0]
    gaussians = geometry.shape[1]
    within = jnp.arange(BLK, dtype=jnp.int32)

    def visit(totals, position):
        grad_geometry, grad_appearance = totals
        camera = position // COLUMNS
        column = position % COLUMNS
        entries = lax.dynamic_slice(block_lists, (camera, column * TPD, jnp.int32(0), jnp.int32(0)), (1, TPD, 2, LIST)).reshape(-1)
        gauss_index = (entries[:, None] * BLK + within[None, :]).reshape(-1)
        raw_params = geometry[:, gauss_index]
        colours = to_half(appearance[:, gauss_index])
        linear = cam_linear[camera]
        camera_shift = cam_shift[camera]
        projected = to_half(project(raw_params, linear, camera_shift))
        cotangent = lax.dynamic_slice(pix_grad, (jnp.int32(0), camera, column * TPD * PIX), (channels, 1, TPD * PIX))
        cotangent = cotangent.reshape(channels, TPD, PIX).astype(jnp.float32)
        picture, grad_proj, grad_colour = tile_grads(projected, colours, cotangent)
        grad_proj = to_half(grad_proj)
        grad_colour = to_half(grad_colour)
        unused, pull_params = jax.vjp(lambda params: project(params, linear, camera_shift), raw_params)
        grad_raw = pull_params(grad_proj)[0]
        grad_geometry = grad_geometry.at[:, gauss_index].add(grad_raw)
        grad_appearance = grad_appearance.at[:, gauss_index].add(grad_colour)
        return ((grad_geometry, grad_appearance), picture.reshape(channels, TPD * PIX))
    initial = (jnp.zeros((6, gaussians), jnp.float32), jnp.zeros((channels, gaussians), jnp.float32))
    totals, pictures = lax.scan(visit, initial, jnp.arange(CAMS * COLUMNS, dtype=jnp.int32))
    rendered = pictures.reshape(CAMS, COLUMNS, channels, TPD * PIX).transpose(2, 0, 1, 3).reshape(channels, CAMS, ITILES * PIX)
    return (rendered, totals[0], totals[1])
```

```python
import functools

import jax
import jax.numpy as jnp
from jax import lax
from jax.experimental import pallas as pl
from jax.experimental.pallas import tpu as pltpu
from jax.sharding import PartitionSpec as P

SIDE = 16
TPD = 16
LIST = 3
BLK = 8
PIX = SIDE * SIDE
LANES = 128
PAR = 32
GEO = 24
STEPS = 2 * LIST * BLK
ROWS = BLK * LANES
MESH = pl.DeviceIdType.MESH
F32 = jnp.float32
BF16 = jnp.bfloat16

NN = (((1,), (0,)), ((), ()))
NT = (((1,), (1,)), ((), ()))
TN = (((0,), (0,)), ((), ()))


def dot(a, b, dims):
    return lax.dot_general(a, b, dims, preferred_element_type=F32)


def iota(shape, dim):
    return lax.broadcasted_iota(jnp.int32, shape, dim)


def rounded(values):
    return values.astype(BF16).astype(F32)


def split(values):
    high = rounded(values)
    rest = values - high
    middle = rounded(rest)
    return high, middle, rest - middle


def project(offset_x, offset_y, diag_x, diag_y, lower, logit, linear, camera_shift):
    lin_xx = 1.0 + linear[0]
    lin_xy = linear[1]
    lin_yx = linear[2]
    lin_yy = 1.0 + linear[3]
    cov_xx = diag_x * diag_x
    cov_xy = diag_x * lower
    cov_yy = lower * lower + diag_y * diag_y
    half_xx = lin_xx * cov_xx + lin_xy * cov_xy
    half_xy = lin_xx * cov_xy + lin_xy * cov_yy
    half_yx = lin_yx * cov_xx + lin_yy * cov_xy
    half_yy = lin_yx * cov_xy + lin_yy * cov_yy
    img_xx = half_xx * lin_xx + half_xy * lin_xy + 0.3
    img_xy = half_xx * lin_yx + half_xy * lin_yy
    img_yy = half_yx * lin_yx + half_yy * lin_yy + 0.3
    determ = img_xx * img_yy - img_xy * img_xy
    centre_x = lin_xx * offset_x + lin_xy * offset_y + camera_shift[0]
    centre_y = lin_yx * offset_x + lin_yy * offset_y + camera_shift[1]
    opacity = 0.95 * jax.nn.sigmoid(logit)
    return (centre_x, centre_y, img_yy / determ, -img_xy / determ, img_xx / determ, opacity)


def kernel(
    tiles,
    cams,
    cap,
    feat,
    params_ref,
    ids_ref,
    linear_ref,
    shift_ref,
    cot_ref,
    picture_ref,
    grads_ref,
    column,
    request_out,
    request_in,
    table_out,
    table_in,
    back_out,
    back_in,
    sums_out,
    sums_in,
    cot,
    lane_sum,
    alpha,
    weight,
    dweight,
    send_cam,
    recv_cam,
    send_req,
    recv_req,
    send_tab,
    recv_tab,
    send_back,
    recv_back,
    send_sum,
    recv_sum,
):
    tile = lax.axis_index("tiles")
    cam = lax.axis_index("cams")
    own = params_ref.shape[1] // BLK
    lanes = own * BLK
    blocks = cams * own
    slots = tiles * cap

    def turn(base, k, size):
        return lax.rem(base + k + size, size)

    barrier = pltpu.get_barrier_semaphore()

    def greet_tiles(k, carry):
        pl.semaphore_signal(
            barrier, inc=1, device_id=(turn(tile, k, tiles), cam), device_id_type=MESH
        )
        return carry

    def greet_cams(k, carry):
        pl.semaphore_signal(
            barrier, inc=1, device_id=(tile, turn(cam, k, cams)), device_id_type=MESH
        )
        return carry

    lax.fori_loop(1, tiles, greet_tiles, 0)
    lax.fori_loop(1, cams, greet_cams, 0)

    ids = ids_ref[...]
    entry_column = lax.div(ids, jnp.int32(blocks))
    in_column = ids - entry_column * blocks
    entry_column = jnp.where(ids < 0, -1, entry_column)
    matches = jnp.where(entry_column == iota((tiles, LANES), 0), 1.0, 0.0)
    earlier = jnp.where(iota((LANES, LANES), 0) < iota((LANES, LANES), 1), 1.0, 0.0)
    before = dot(matches.astype(BF16), earlier.astype(BF16), NN)
    rank = jnp.sum(before * matches, axis=0, keepdims=True).astype(jnp.int32)
    slot = jnp.where(ids < 0, -1, entry_column * cap + rank)
    slot_hot = jnp.where(slot == iota((slots, LANES), 0), 1.0, 0.0).astype(BF16)
    block_hot = jnp.where(in_column == iota((blocks, LANES), 0), 1.0, 0.0).astype(BF16)
    request_out[...] = dot(slot_hot, block_hot, NT).astype(BF16).reshape(tiles, cap, blocks)

    def cam_copy(source, target, k, sends, recvs):
        return pltpu.make_async_remote_copy(
            src_ref=source,
            dst_ref=target,
            send_sem=sends.at[k],
            recv_sem=recvs.at[k],
            device_id=(tile, turn(cam, k, cams)),
            device_id_type=MESH,
        )

    def tile_copy(source, target, k, sends, recvs):
        peer = turn(tile, k, tiles)
        return pltpu.make_async_remote_copy(
            src_ref=source.at[peer],
            dst_ref=target.at[tile],
            send_sem=sends.at[k],
            recv_sem=recvs.at[k],
            device_id=(peer, cam),
            device_id_type=MESH,
        )

    def over(size, make, what):
        def step(k, carry):
            getattr(make(k), what)()
            return carry

        lax.fori_loop(1, size, step, 0)

    copy_params = lambda k: cam_copy(params_ref, column.at[cam], k, send_cam, recv_cam)
    copy_request = lambda k: tile_copy(request_out, request_in, k, send_req, recv_req)
    copy_table = lambda k: tile_copy(table_out, table_in, k, send_tab, recv_tab)
    copy_back = lambda k: tile_copy(back_out, back_in, k, send_back, recv_back)
    copy_sums = lambda k: cam_copy(
        sums_out.at[turn(cam, k, cams)], sums_in.at[cam], k, send_sum, recv_sum
    )

    pl.semaphore_wait(barrier, tiles - 1 + cams - 1)
    over(cams, copy_params, "start")
    over(tiles, copy_request, "start")
    column[cam] = params_ref[...]
    request_in[tile] = request_out[tile]

    fill = jnp.zeros((PAR - feat, PIX), F32)
    for t in range(TPD):
        part = cot_ref[:, t * PIX : (t + 1) * PIX].astype(F32)
        cot[t * PAR : (t + 1) * PAR] = jnp.concatenate([part, fill], axis=0).astype(BF16)
    pixel = iota((1, PIX), 1)
    across = (pixel & (SIDE - 1)).astype(F32) + (0.5 - SIDE / 2)
    downward = lax.div(pixel, jnp.int32(SIDE)).astype(F32) + (0.5 - SIDE / 2)
    one = jnp.ones((1, PIX), F32)
    none = jnp.zeros((2, PIX), F32)
    mono = jnp.concatenate(
        [one, across, downward, across * across, across * downward, downward * downward, none],
        axis=0,
    )
    mono_three = jnp.concatenate([mono, mono, mono, jnp.zeros((8, PIX), F32)], axis=0).astype(BF16)
    mono_one = jnp.concatenate([mono, jnp.zeros((8, PIX), F32)], axis=0).astype(BF16)
    spread = jnp.where(
        (iota((PAR, TPD * PAR), 1) & (PAR - 1)) == iota((PAR, TPD * PAR), 0), 1.0, 0.0
    ).astype(BF16)

    over(cams, copy_params, "wait_recv")
    split_rows = GEO + 3 * (PAR - GEO)
    in_block = iota((split_rows, BLK, lanes), 2) & (BLK - 1)
    in_place = in_block == iota((split_rows, BLK, lanes), 1)
    table = jnp.zeros((split_rows * BLK, blocks), F32)
    for c in range(cams):
        piece = column[c]
        stacked = jnp.concatenate([piece[:GEO], *split(piece[GEO:])], axis=0)
        apart = jnp.where(in_place, jnp.broadcast_to(stacked[:, None, :], in_place.shape), 0.0)
        apart = apart.reshape(split_rows * BLK, lanes).astype(BF16)
        to_block = jnp.where(
            iota((lanes, blocks), 1) == c * own + lax.div(iota((lanes, blocks), 0), jnp.int32(BLK)),
            1.0,
            0.0,
        ).astype(BF16)
        table = table + dot(apart, to_block, NN)
    geo_rows = (PAR - GEO) * BLK
    base = GEO * BLK
    geometry = (
        table[base : base + geo_rows]
        + table[base + geo_rows : base + 2 * geo_rows]
        + table[base + 2 * geo_rows :]
    )
    geometry = [geometry[r * BLK : (r + 1) * BLK] for r in range(6)]
    linear = [linear_ref[0, i] for i in range(4)]
    camera_shift = [shift_ref[0, i] for i in range(2)]
    projected, pull_params = jax.vjp(lambda *rows: project(*rows, linear, camera_shift), *geometry)
    table = jnp.concatenate(
        [table[:base], *projected, jnp.zeros((2 * BLK, blocks), F32)], axis=0
    ).astype(BF16)

    over(tiles, copy_request, "wait_recv")
    wanted = request_in[...].reshape(slots, blocks)
    table_out[...] = dot(wanted, table, NT).astype(BF16).reshape(tiles, cap, PAR * BLK)
    over(tiles, copy_table, "start")
    table_in[tile] = table_out[tile]
    empty = jnp.zeros((2 * TPD, PIX), F32)
    for g in range(BLK):
        row = g * LANES + 2 * LIST * TPD
        weight[row : row + 2 * TPD] = empty
        dweight[row : row + 2 * TPD] = empty
    over(tiles, copy_table, "wait_recv")

    lane_sum[...] = dot(table_in[...].reshape(slots, PAR * BLK), slot_hot, TN)
    copies = jnp.concatenate([lane_sum[pl.ds(g, PAR, stride=BLK), :] for g in range(BLK)], axis=1)
    same_tile = (iota((TPD, 1, ROWS), 2) & (TPD - 1)) == iota((TPD, 1, ROWS), 0)
    u_x, u_y, con_x, con_m, con_y, opacity = [
        copies[GEO + r : GEO + r + 1] for r in range(6)
    ]
    opacity = jnp.where(opacity > 0.0, opacity, 1.0)
    slope_x = con_x * u_x + con_m * u_y
    slope_y = con_m * u_x + con_y * u_y
    poly = jnp.concatenate(
        [
            jnp.log(opacity) - 0.5 * (slope_x * u_x + slope_y * u_y),
            slope_x,
            slope_y,
            -0.5 * con_x,
            -con_m,
            -0.5 * con_y,
            jnp.zeros((2, ROWS), F32),
        ],
        axis=0,
    )
    poly = jnp.concatenate([*split(poly), jnp.zeros((8, ROWS), F32)], axis=0).astype(BF16)
    alpha[...] = dot(poly, mono_three, TN)
    keep = jnp.ones((TPD, PIX), F32)
    order = [g * LANES + j * TPD for j in range(2 * LIST) for g in range(BLK)]
    for row in order:
        cover = jnp.exp(alpha[row : row + TPD])
        share = keep * cover
        keep = keep - share
        alpha[row : row + TPD] = cover
        weight[row : row + TPD] = share

    colour_rows = dot(copies.T.astype(BF16), spread, NN)
    own_tile = lax.div(iota((ROWS, TPD * PAR), 1), jnp.int32(PAR)) == (
        iota((ROWS, TPD * PAR), 0) & (TPD - 1)
    )
    colour_rows = jnp.where(own_tile, colour_rows, 0.0).astype(BF16)
    dweight_all = dot(colour_rows, cot[...], NN)
    behind = jnp.zeros((TPD, PIX), F32)
    for row in reversed(order):
        gap = dweight_all[row : row + TPD] - behind
        dweight[row : row + TPD] = weight[row : row + TPD] * gap
        behind = behind + alpha[row : row + TPD] * gap

    shares = weight[...].astype(BF16)
    pulled = dweight[...]
    pulled_high = pulled.astype(BF16)
    pulled_low = (pulled - pulled_high.astype(F32)).astype(BF16)
    moment = dot(mono_one, pulled_high, NT) + dot(mono_one, pulled_low, NT)
    m_0, m_x, m_y, m_xx, m_xy, m_yy = [moment[r : r + 1] for r in range(6)]
    s_x = m_x - u_x * m_0
    s_y = m_y - u_y * m_0
    s_xx = m_xx - u_x * (m_x + s_x)
    s_xy = m_xy - u_x * m_y - u_y * s_x
    s_yy = m_yy - u_y * (m_y + s_y)
    by_tile = dot(cot[...], shares, NT).reshape(TPD, PAR, ROWS)
    colour_grads = jnp.sum(jnp.where(same_tile, by_tile, 0.0), axis=0)
    copy_grads = jnp.concatenate(
        [
            colour_grads[:GEO],
            con_x * s_x + con_m * s_y,
            con_m * s_x + con_y * s_y,
            -0.5 * s_xx,
            -s_xy,
            -0.5 * s_yy,
            m_0 / opacity,
            jnp.zeros((2, ROWS), F32),
        ],
        axis=0,
    )
    for g in range(BLK):
        lane_sum[pl.ds(g, PAR, stride=BLK), :] = copy_grads[:, g * LANES : (g + 1) * LANES]
    back = dot(slot_hot, lane_sum[...].astype(BF16), NT)
    back_out[...] = back.astype(BF16).reshape(tiles, cap, PAR * BLK)
    over(tiles, copy_back, "start")
    back_in[tile] = back_out[tile]

    masked = jnp.where(same_tile, jnp.broadcast_to(copies[None], (TPD, PAR, ROWS)), 0.0)
    picture = dot(masked.reshape(TPD * PAR, ROWS).astype(BF16), shares, NN)
    for t in range(TPD):
        picture_ref[:, t * PIX : (t + 1) * PIX] = picture[t * PAR : t * PAR + feat]

    over(tiles, copy_back, "wait_recv")
    summed = dot(back_in[...].reshape(slots, PAR * BLK), wanted, TN)
    pulled_geo = pull_params(
        tuple(summed[base + r * BLK : base + (r + 1) * BLK] for r in range(6))
    )
    block_grads = jnp.concatenate(
        [summed[:base], *pulled_geo, jnp.zeros((2 * BLK, blocks), F32)], axis=0
    )
    parts = jnp.concatenate(split(block_grads), axis=0).astype(BF16)
    place = iota((PAR, lanes), 1) & (BLK - 1)
    for c in range(cams):
        from_block = jnp.where(
            iota((blocks, lanes), 0) == c * own + lax.div(iota((blocks, lanes), 1), jnp.int32(BLK)),
            1.0,
            0.0,
        ).astype(BF16)
        apart = dot(parts, from_block, NN)
        rows = PAR * BLK
        apart = apart[:rows] + apart[rows : 2 * rows] + apart[2 * rows :]
        apart = apart.reshape(PAR, BLK, lanes)
        chosen = jnp.where(
            (iota((PAR, BLK, lanes), 2) & (BLK - 1)) == iota((PAR, BLK, lanes), 1), apart, 0.0
        )
        sums_out[c] = jnp.sum(chosen, axis=1)
    over(cams, copy_sums, "start")
    sums_in[cam] = sums_out[cam]
    over(cams, copy_sums, "wait_recv")
    grads_ref[...] = jnp.sum(sums_in[...], axis=0)

    over(cams, copy_params, "wait_send")
    over(tiles, copy_request, "wait_send")
    over(tiles, copy_table, "wait_send")
    over(tiles, copy_back, "wait_send")
    over(cams, copy_sums, "wait_send")


def local(
    offsets,
    factor_diag,
    factor_off,
    logit,
    appearance,
    cam_linear,
    cam_shift,
    block_lists,
    pix_grad,
):
    tiles = lax.axis_size("tiles")
    cams = lax.axis_size("cams")
    channels = appearance.shape[0]
    lanes = offsets.shape[1]
    blocks = cams * lanes // BLK
    cap = -(-(4 * TPD * LIST // tiles) // 16) * 16
    params = jnp.concatenate(
        [
            appearance,
            jnp.zeros((GEO - channels, lanes), F32),
            offsets,
            factor_diag,
            factor_off[None, :],
            logit[None, :],
            jnp.zeros((PAR - GEO - 6, lanes), F32),
        ],
        axis=0,
    )
    ids = block_lists.reshape(TPD, 2 * LIST).T.reshape(1, TPD * 2 * LIST)
    ids = jnp.pad(ids, ((0, 0), (0, LANES - ids.shape[1])), constant_values=-1)
    vmem = pl.BlockSpec(memory_space=pltpu.VMEM)
    smem = pl.BlockSpec(memory_space=pltpu.SMEM)
    row = PAR * BLK
    dma = pltpu.SemaphoreType.DMA
    picture, grads = pl.pallas_call(
        functools.partial(kernel, tiles, cams, cap, channels),
        out_shape=(
            jax.ShapeDtypeStruct((channels, TPD * PIX), F32),
            jax.ShapeDtypeStruct((PAR, lanes), F32),
        ),
        in_specs=[vmem, vmem, smem, smem, vmem],
        out_specs=(vmem, vmem),
        scratch_shapes=[
            pltpu.VMEM((cams, PAR, lanes), F32),
            pltpu.VMEM((tiles, cap, blocks), BF16),
            pltpu.VMEM((tiles, cap, blocks), BF16),
            pltpu.VMEM((tiles, cap, row), BF16),
            pltpu.VMEM((tiles, cap, row), BF16),
            pltpu.VMEM((tiles, cap, row), BF16),
            pltpu.VMEM((tiles, cap, row), BF16),
            pltpu.VMEM((cams, PAR, lanes), F32),
            pltpu.VMEM((cams, PAR, lanes), F32),
            pltpu.VMEM((TPD * PAR, PIX), BF16),
            pltpu.VMEM((row, LANES), F32),
            pltpu.VMEM((ROWS, PIX), F32),
            pltpu.VMEM((ROWS, PIX), F32),
            pltpu.VMEM((ROWS, PIX), F32),
            dma((cams,)),
            dma((cams,)),
            dma((tiles,)),
            dma((tiles,)),
            dma((tiles,)),
            dma((tiles,)),
            dma((tiles,)),
            dma((tiles,)),
            dma((cams,)),
            dma((cams,)),
        ],
        compiler_params=pltpu.CompilerParams(
            collective_id=0, has_side_effects=True, vmem_limit_bytes=48 * 1024 * 1024
        ),
    )(params, ids, cam_linear, cam_shift, pix_grad.reshape(channels, TPD * PIX))
    return (
        picture.reshape(channels, 1, TPD * PIX),
        grads[GEO : GEO + 6],
        grads[:channels],
    )


def solution(mesh):
    return jax.shard_map(
        local,
        mesh=mesh,
        in_specs=(
            P(None, ("tiles", "cams")),
            P(None, ("tiles", "cams")),
            P(("tiles", "cams")),
            P(("tiles", "cams")),
            P(None, ("tiles", "cams")),
            P("cams", None),
            P("cams", None),
            P("cams", "tiles", None, None),
            P(None, "cams", "tiles"),
        ),
        out_specs=(
            P(None, "cams", "tiles"),
            P(None, ("tiles", "cams")),
            P(None, ("tiles", "cams")),
        ),
        check_vma=False,
    )
```

```python
import functools

import jax
import jax.numpy as jnp
from jax import lax
from jax.experimental import pallas as pl
from jax.experimental.pallas import tpu as pltpu
from jax.sharding import PartitionSpec as P

SIDE = 16
TPD = 16
LIST = 3
BLK = 8
PIX = SIDE * SIDE
LANES = 128
PAR = 32
GEO = 24
STEPS = 2 * LIST * BLK
ROWS = BLK * LANES
MESH = pl.DeviceIdType.MESH
F32 = jnp.float32
BF16 = jnp.bfloat16

NN = (((1,), (0,)), ((), ()))
NT = (((1,), (1,)), ((), ()))
TN = (((0,), (0,)), ((), ()))


def dot(a, b, dims):
    return lax.dot_general(a, b, dims, preferred_element_type=F32)


def iota(shape, dim):
    return lax.broadcasted_iota(jnp.int32, shape, dim)


def rounded(values):
    return values.astype(BF16).astype(F32)


def split(values):
    high = rounded(values)
    rest = values - high
    middle = rounded(rest)
    return high, middle, rest - middle


def project(offset_x, offset_y, diag_x, diag_y, lower, logit, linear, camera_shift):
    lin_xx = 1.0 + linear[0]
    lin_xy = linear[1]
    lin_yx = linear[2]
    lin_yy = 1.0 + linear[3]
    cov_xx = diag_x * diag_x
    cov_xy = diag_x * lower
    cov_yy = lower * lower + diag_y * diag_y
    half_xx = lin_xx * cov_xx + lin_xy * cov_xy
    half_xy = lin_xx * cov_xy + lin_xy * cov_yy
    half_yx = lin_yx * cov_xx + lin_yy * cov_xy
    half_yy = lin_yx * cov_xy + lin_yy * cov_yy
    img_xx = half_xx * lin_xx + half_xy * lin_xy + 0.3
    img_xy = half_xx * lin_yx + half_xy * lin_yy
    img_yy = half_yx * lin_yx + half_yy * lin_yy + 0.3
    determ = img_xx * img_yy - img_xy * img_xy
    centre_x = lin_xx * offset_x + lin_xy * offset_y + camera_shift[0]
    centre_y = lin_yx * offset_x + lin_yy * offset_y + camera_shift[1]
    opacity = 0.95 * jax.nn.sigmoid(logit)
    return (centre_x, centre_y, img_yy / determ, -img_xy / determ, img_xx / determ, opacity)


def kernel(
    tiles,
    cams,
    cap,
    feat,
    *refs,
):
    hbm_in = refs[:9]
    picture_ref, geometry_ref, appearance_ref = refs[9:12]
    held_in = refs[12:21]
    offsets_ref, diag_ref, lower_ref, logit_ref, looks_ref = held_in[:5]
    linear_ref, shift_ref, lists_ref, cot_ref = held_in[5:]
    body(
        tiles, cams, cap, feat, hbm_in, held_in, offsets_ref, diag_ref, lower_ref, logit_ref,
        looks_ref, linear_ref, shift_ref, lists_ref, cot_ref, picture_ref, geometry_ref,
        appearance_ref, *refs[21:]
    )


def body(
    tiles,
    cams,
    cap,
    feat,
    hbm_in,
    held_in,
    offsets_ref,
    diag_ref,
    lower_ref,
    logit_ref,
    looks_ref,
    linear_ref,
    shift_ref,
    lists_ref,
    cot_ref,
    picture_ref,
    geometry_ref,
    appearance_ref,
    load_sem,
    params_ref,
    column,
    request_out,
    request_in,
    table_out,
    table_in,
    back_out,
    back_in,
    sums_out,
    sums_in,
    cot,
    lane_sum,
    alpha,
    weight,
    dweight,
    send_cam,
    recv_cam,
    send_req,
    recv_req,
    send_tab,
    recv_tab,
    send_back,
    recv_back,
    send_sum,
    recv_sum,
):
    tile = lax.axis_index("tiles")
    cam = lax.axis_index("cams")
    own = params_ref.shape[1] // BLK
    lanes = own * BLK
    blocks = cams * own
    slots = tiles * cap

    def turn(base, k, size):
        return lax.rem(base + k + size, size)

    barrier = pltpu.get_barrier_semaphore()

    def greet_tiles(k, carry):
        pl.semaphore_signal(
            barrier, inc=1, device_id=(turn(tile, k, tiles), cam), device_id_type=MESH
        )
        return carry

    def greet_cams(k, carry):
        pl.semaphore_signal(
            barrier, inc=1, device_id=(tile, turn(cam, k, cams)), device_id_type=MESH
        )
        return carry

    lax.fori_loop(1, tiles, greet_tiles, 0)
    lax.fori_loop(1, cams, greet_cams, 0)

    loads = [
        pltpu.make_async_copy(source, target, load_sem.at[i])
        for i, (source, target) in enumerate(zip(hbm_in, held_in))
    ]
    for i in (7, 0, 1, 2, 3, 4, 5, 6, 8):
        loads[i].start()

    loads[7].wait()
    ids = jnp.concatenate(
        [lists_ref[l, d : d + 1, :] for d in range(2) for l in range(LIST)]
        + [jnp.full((1, LANES - 2 * LIST * TPD), -1, jnp.int32)],
        axis=1,
    )
    entry_column = lax.div(ids, jnp.int32(blocks))
    in_column = ids - entry_column * blocks
    entry_column = jnp.where(ids < 0, -1, entry_column)
    matches = jnp.where(entry_column == iota((tiles, LANES), 0), 1.0, 0.0)
    earlier = jnp.where(iota((LANES, LANES), 0) < iota((LANES, LANES), 1), 1.0, 0.0)
    before = dot(matches.astype(BF16), earlier.astype(BF16), NN)
    rank = jnp.sum(before * matches, axis=0, keepdims=True).astype(jnp.int32)
    slot = jnp.where(ids < 0, -1, entry_column * cap + rank)
    slot_hot = jnp.where(slot == iota((slots, LANES), 0), 1.0, 0.0).astype(BF16)
    block_hot = jnp.where(in_column == iota((blocks, LANES), 0), 1.0, 0.0).astype(BF16)
    request_out[...] = dot(slot_hot, block_hot, NT).astype(BF16).reshape(tiles, cap, blocks)

    def cam_copy(source, target, k, sends, recvs):
        return pltpu.make_async_remote_copy(
            src_ref=source,
            dst_ref=target,
            send_sem=sends.at[k],
            recv_sem=recvs.at[k],
            device_id=(tile, turn(cam, k, cams)),
            device_id_type=MESH,
        )

    def tile_copy(source, target, k, sends, recvs):
        peer = turn(tile, k, tiles)
        return pltpu.make_async_remote_copy(
            src_ref=source.at[peer],
            dst_ref=target.at[tile],
            send_sem=sends.at[k],
            recv_sem=recvs.at[k],
            device_id=(peer, cam),
            device_id_type=MESH,
        )

    def over(size, make, what):
        def step(k, carry):
            getattr(make(k), what)()
            return carry

        lax.fori_loop(1, size, step, 0)

    copy_params = lambda k: cam_copy(params_ref, column.at[cam], k, send_cam, recv_cam)
    copy_request = lambda k: tile_copy(request_out, request_in, k, send_req, recv_req)
    copy_table = lambda k: tile_copy(table_out, table_in, k, send_tab, recv_tab)
    copy_back = lambda k: tile_copy(back_out, back_in, k, send_back, recv_back)
    copy_sums = lambda k: cam_copy(
        sums_out.at[turn(cam, k, cams)], sums_in.at[cam], k, send_sum, recv_sum
    )

    for i in range(5):
        loads[i].wait()
    looks = looks_ref[...]
    geometry = jnp.concatenate(
        [offsets_ref[...], diag_ref[...], lower_ref[...], logit_ref[...], jnp.zeros((2, lanes), F32)],
        axis=0,
    )
    params_ref[...] = jnp.concatenate(
        [looks, jnp.zeros((GEO - feat, lanes), F32), *split(geometry)], axis=0
    ).astype(BF16)
    pl.semaphore_wait(barrier, tiles - 1 + cams - 1)
    over(cams, copy_params, "start")
    over(tiles, copy_request, "start")
    column[cam] = params_ref[...]
    request_in[tile] = request_out[tile]

    loads[8].wait()
    fill = jnp.zeros((PAR - feat, PIX), F32)
    for t in range(TPD):
        part = cot_ref[:, t * PIX : (t + 1) * PIX].astype(F32)
        cot[t * PAR : (t + 1) * PAR] = jnp.concatenate([part, fill], axis=0).astype(BF16)
    pixel = iota((1, PIX), 1)
    across = (pixel & (SIDE - 1)).astype(F32) + (0.5 - SIDE / 2)
    downward = lax.div(pixel, jnp.int32(SIDE)).astype(F32) + (0.5 - SIDE / 2)
    one = jnp.ones((1, PIX), F32)
    none = jnp.zeros((2, PIX), F32)
    mono = jnp.concatenate(
        [one, across, downward, across * across, across * downward, downward * downward, none],
        axis=0,
    )
    mono_three = jnp.concatenate([mono, mono, mono, jnp.zeros((8, PIX), F32)], axis=0).astype(BF16)
    mono_one = jnp.concatenate([mono, jnp.zeros((8, PIX), F32)], axis=0).astype(BF16)
    spread = jnp.where(
        (iota((PAR, TPD * PAR), 1) & (PAR - 1)) == iota((PAR, TPD * PAR), 0), 1.0, 0.0
    ).astype(BF16)

    loads[5].wait()
    loads[6].wait()
    over(cams, copy_params, "wait_recv")
    split_rows = GEO + 3 * (PAR - GEO)
    in_block = iota((split_rows, BLK, lanes), 2) & (BLK - 1)
    in_place = in_block == iota((split_rows, BLK, lanes), 1)
    table = jnp.zeros((split_rows * BLK, blocks), F32)
    for c in range(cams):
        stacked = column[c].astype(F32)
        apart = jnp.where(in_place, jnp.broadcast_to(stacked[:, None, :], in_place.shape), 0.0)
        apart = apart.reshape(split_rows * BLK, lanes).astype(BF16)
        to_block = jnp.where(
            iota((lanes, blocks), 1) == c * own + lax.div(iota((lanes, blocks), 0), jnp.int32(BLK)),
            1.0,
            0.0,
        ).astype(BF16)
        table = table + dot(apart, to_block, NN)
    geo_rows = (PAR - GEO) * BLK
    base = GEO * BLK
    geometry = (
        table[base : base + geo_rows]
        + table[base + geo_rows : base + 2 * geo_rows]
        + table[base + 2 * geo_rows :]
    )
    geometry = [geometry[r * BLK : (r + 1) * BLK] for r in range(6)]
    linear = [linear_ref[:, i : i + 1] for i in range(4)]
    camera_shift = [shift_ref[:, i : i + 1] for i in range(2)]
    projected, pull_params = jax.vjp(lambda *rows: project(*rows, linear, camera_shift), *geometry)
    table = jnp.concatenate(
        [table[:base], *projected, jnp.zeros((2 * BLK, blocks), F32)], axis=0
    ).astype(BF16)

    over(tiles, copy_request, "wait_recv")
    wanted = request_in[...].reshape(slots, blocks)
    table_out[...] = dot(wanted, table, NT).astype(BF16).reshape(tiles, cap, PAR * BLK)
    over(tiles, copy_table, "start")
    table_in[tile] = table_out[tile]
    empty = jnp.zeros((2 * TPD, PIX), F32)
    for g in range(BLK):
        row = g * LANES + 2 * LIST * TPD
        weight[row : row + 2 * TPD] = empty
        dweight[row : row + 2 * TPD] = empty
    over(tiles, copy_table, "wait_recv")

    lane_sum[...] = dot(table_in[...].reshape(slots, PAR * BLK), slot_hot, TN)
    copies = jnp.concatenate([lane_sum[pl.ds(g, PAR, stride=BLK), :] for g in range(BLK)], axis=1)
    same_tile = (iota((TPD, 1, ROWS), 2) & (TPD - 1)) == iota((TPD, 1, ROWS), 0)
    u_x, u_y, con_x, con_m, con_y, opacity = [
        copies[GEO + r : GEO + r + 1] for r in range(6)
    ]
    opacity = jnp.where(opacity > 0.0, opacity, 1.0)
    slope_x = con_x * u_x + con_m * u_y
    slope_y = con_m * u_x + con_y * u_y
    poly = jnp.concatenate(
        [
            jnp.log(opacity) - 0.5 * (slope_x * u_x + slope_y * u_y),
            slope_x,
            slope_y,
            -0.5 * con_x,
            -con_m,
            -0.5 * con_y,
            jnp.zeros((2, ROWS), F32),
        ],
        axis=0,
    )
    poly = jnp.concatenate([*split(poly), jnp.zeros((8, ROWS), F32)], axis=0).astype(BF16)
    alpha[...] = dot(poly, mono_three, TN)
    keep = jnp.ones((TPD, PIX), F32)
    order = [g * LANES + j * TPD for j in range(2 * LIST) for g in range(BLK)]
    for row in order:
        cover = jnp.exp(alpha[row : row + TPD])
        share = keep * cover
        keep = keep - share
        alpha[row : row + TPD] = cover
        weight[row : row + TPD] = share

    colour_rows = dot(copies.T.astype(BF16), spread, NN)
    own_tile = lax.div(iota((ROWS, TPD * PAR), 1), jnp.int32(PAR)) == (
        iota((ROWS, TPD * PAR), 0) & (TPD - 1)
    )
    colour_rows = jnp.where(own_tile, colour_rows, 0.0).astype(BF16)
    dweight_all = dot(colour_rows, cot[...], NN)
    behind = jnp.zeros((TPD, PIX), F32)
    for row in reversed(order):
        gap = dweight_all[row : row + TPD] - behind
        dweight[row : row + TPD] = weight[row : row + TPD] * gap
        behind = behind + alpha[row : row + TPD] * gap

    shares = weight[...].astype(BF16)
    pulled = dweight[...]
    pulled_high = pulled.astype(BF16)
    pulled_low = (pulled - pulled_high.astype(F32)).astype(BF16)
    moment = dot(mono_one, pulled_high, NT) + dot(mono_one, pulled_low, NT)
    m_0, m_x, m_y, m_xx, m_xy, m_yy = [moment[r : r + 1] for r in range(6)]
    s_x = m_x - u_x * m_0
    s_y = m_y - u_y * m_0
    s_xx = m_xx - u_x * (m_x + s_x)
    s_xy = m_xy - u_x * m_y - u_y * s_x
    s_yy = m_yy - u_y * (m_y + s_y)
    by_tile = dot(cot[...], shares, NT).reshape(TPD, PAR, ROWS)
    colour_grads = jnp.sum(jnp.where(same_tile, by_tile, 0.0), axis=0)
    copy_grads = jnp.concatenate(
        [
            colour_grads[:GEO],
            con_x * s_x + con_m * s_y,
            con_m * s_x + con_y * s_y,
            -0.5 * s_xx,
            -s_xy,
            -0.5 * s_yy,
            m_0 / opacity,
            jnp.zeros((2, ROWS), F32),
        ],
        axis=0,
    )
    for g in range(BLK):
        lane_sum[pl.ds(g, PAR, stride=BLK), :] = copy_grads[:, g * LANES : (g + 1) * LANES]
    back = dot(slot_hot, lane_sum[...].astype(BF16), NT)
    back_out[...] = back.astype(BF16).reshape(tiles, cap, PAR * BLK)
    over(tiles, copy_back, "start")
    back_in[tile] = back_out[tile]

    masked = jnp.where(same_tile, jnp.broadcast_to(copies[None], (TPD, PAR, ROWS)), 0.0)
    picture = dot(masked.reshape(TPD * PAR, ROWS).astype(BF16), shares, NN)
    for t in range(TPD):
        picture_ref[:, 0, t * PIX : (t + 1) * PIX] = picture[t * PAR : t * PAR + feat]

    over(tiles, copy_back, "wait_recv")
    summed = dot(back_in[...].reshape(slots, PAR * BLK), wanted, TN)
    pulled_geo = pull_params(
        tuple(summed[base + r * BLK : base + (r + 1) * BLK] for r in range(6))
    )
    block_grads = jnp.concatenate(
        [summed[:base], *pulled_geo, jnp.zeros((2 * BLK, blocks), F32)], axis=0
    )
    parts = jnp.concatenate(split(block_grads), axis=0).astype(BF16)
    place = iota((PAR, lanes), 1) & (BLK - 1)
    for c in range(cams):
        from_block = jnp.where(
            iota((blocks, lanes), 0) == c * own + lax.div(iota((blocks, lanes), 1), jnp.int32(BLK)),
            1.0,
            0.0,
        ).astype(BF16)
        apart = dot(parts, from_block, NN)
        rows = PAR * BLK
        apart = apart[:rows] + apart[rows : 2 * rows] + apart[2 * rows :]
        apart = apart.reshape(PAR, BLK, lanes)
        chosen = jnp.where(
            (iota((PAR, BLK, lanes), 2) & (BLK - 1)) == iota((PAR, BLK, lanes), 1), apart, 0.0
        )
        sums_out[c] = jnp.sum(chosen, axis=1)
    over(cams, copy_sums, "start")
    sums_in[cam] = sums_out[cam]
    over(cams, copy_sums, "wait_recv")
    total = jnp.sum(sums_in[...], axis=0)
    geometry_ref[...] = total[GEO : GEO + 6]
    appearance_ref[...] = total[:feat]

    over(cams, copy_params, "wait_send")
    over(tiles, copy_request, "wait_send")
    over(tiles, copy_table, "wait_send")
    over(tiles, copy_back, "wait_send")
    over(cams, copy_sums, "wait_send")


def store(*refs):
    sems = refs[6]
    copies = [pltpu.make_async_copy(refs[i], refs[3 + i], sems.at[i]) for i in range(3)]
    for copy in copies:
        copy.start()
    for copy in copies:
        copy.wait()


def local(
    offsets,
    factor_diag,
    factor_off,
    logit,
    appearance,
    cam_linear,
    cam_shift,
    block_lists,
    pix_grad,
):
    tiles = lax.axis_size("tiles")
    cams = lax.axis_size("cams")
    channels = appearance.shape[0]
    lanes = offsets.shape[1]
    blocks = cams * lanes // BLK
    cap = -(-(4 * TPD * LIST // tiles) // 16) * 16
    vmem = pl.BlockSpec(memory_space=pltpu.VMEM)
    hbm = pl.BlockSpec(memory_space=pltpu.HBM)
    arrays = (
        offsets,
        factor_diag,
        factor_off[None, :],
        logit[None, :],
        appearance,
        cam_linear,
        cam_shift,
        block_lists.transpose(0, 3, 2, 1).reshape(LIST, 2, TPD),
        pix_grad.reshape(channels, TPD * PIX),
    )
    split_rows = GEO + 3 * (PAR - GEO)
    row = PAR * BLK
    dma = pltpu.SemaphoreType.DMA
    results = pl.pallas_call(
        functools.partial(kernel, tiles, cams, cap, channels),
        out_shape=(
            jax.ShapeDtypeStruct((channels, 1, TPD * PIX), F32),
            jax.ShapeDtypeStruct((6, lanes), F32),
            jax.ShapeDtypeStruct((channels, lanes), F32),
        ),
        in_specs=[hbm] * len(arrays),
        out_specs=(vmem,) * 3,
        scratch_shapes=[
            *[pltpu.VMEM(array.shape, array.dtype) for array in arrays],
            dma((len(arrays),)),
            pltpu.VMEM((split_rows, lanes), BF16),
            pltpu.VMEM((cams, split_rows, lanes), BF16),
            pltpu.VMEM((tiles, cap, blocks), BF16),
            pltpu.VMEM((tiles, cap, blocks), BF16),
            pltpu.VMEM((tiles, cap, row), BF16),
            pltpu.VMEM((tiles, cap, row), BF16),
            pltpu.VMEM((tiles, cap, row), BF16),
            pltpu.VMEM((tiles, cap, row), BF16),
            pltpu.VMEM((cams, PAR, lanes), F32),
            pltpu.VMEM((cams, PAR, lanes), F32),
            pltpu.VMEM((TPD * PAR, PIX), BF16),
            pltpu.VMEM((row, LANES), F32),
            pltpu.VMEM((ROWS, PIX), F32),
            pltpu.VMEM((ROWS, PIX), F32),
            pltpu.VMEM((ROWS, PIX), F32),
            dma((cams,)),
            dma((cams,)),
            dma((tiles,)),
            dma((tiles,)),
            dma((tiles,)),
            dma((tiles,)),
            dma((tiles,)),
            dma((tiles,)),
            dma((cams,)),
            dma((cams,)),
        ],
        compiler_params=pltpu.CompilerParams(
            collective_id=0, has_side_effects=True, vmem_limit_bytes=64 * 1024 * 1024
        ),
    )(*arrays)
    return pl.pallas_call(
        store,
        out_shape=tuple(jax.ShapeDtypeStruct(r.shape, r.dtype) for r in results),
        in_specs=[vmem] * 3,
        out_specs=(hbm,) * 3,
        scratch_shapes=[dma((3,))],
    )(*results)


def solution(mesh):
    return jax.shard_map(
        local,
        mesh=mesh,
        in_specs=(
            P(None, ("tiles", "cams")),
            P(None, ("tiles", "cams")),
            P(("tiles", "cams")),
            P(("tiles", "cams")),
            P(None, ("tiles", "cams")),
            P("cams", None),
            P("cams", None),
            P("cams", "tiles", None, None),
            P(None, "cams", "tiles"),
        ),
        out_specs=(
            P(None, "cams", "tiles"),
            P(None, ("tiles", "cams")),
            P(None, ("tiles", "cams")),
        ),
        check_vma=False,
    )
```
